32 devices in a mesh: atom: 8 (over z, y), energy: 4 (over x, core).
Axes of the slice: x: 2, y: 2, z: 4, core: 2. Of those that a mesh axis runs over, the one named last changes fastest.
Arguments:
- green: bfloat16 [16, 2, 12, 12, 512], P('atom', None, None, None, 'energy'), may hold values from -6 to 6
- coupling: bfloat16 [16, 34, 2, 12, 12], P('atom'), may hold values from -0.5 to 0.5
- neighbours: int32 [16, 34], P('atom'), may hold values from 0 to 15, as said below
- offsets: int32 [70], replicated, may hold values from 1 to 48, as said below
- w_emit: float32 [70], replicated, may hold values from 0.02 to 0.2
- w_absorb: float32 [70], replicated, may hold values from 0.02 to 0.2
Outputs:
- self_energy: float32 [16, 2, 12, 12, 512], P('atom', None, None, None, 'energy')
The draws below stay inside these ranges and needn't reach their ends.
Inputs may be any that keep to these rules, and one draw needn't show every extreme that they name: neighbours[a, k] lies among the atoms a // 2 - 1, a // 2, a // 2 + 1 times 2 plus 0 to 1, that is, among the atoms of the same index of atom or of an index one away. `offsets`: some frequency equals 48.
All inputs are finite; a program needn't handle non-finite values.
Results may differ from the reference program's by a relative error of at most 0.0028.
Values may be sent and summed in bfloat16 or wider, within the bound.
A program may use at most 64 MiB of HBM per device.

```python
import math
import jax
import jax.numpy as jnp
from jax import lax

ORB = 12
NB = 34
NQ = 70
A_DEV = 2
OMAX = 48
ATOMS = 16
EN = 512


def draw_neighbours(key, part):
    count = ATOMS // A_DEV
    keys = jax.random.split(jax.random.fold_in(key, 11), 4)
    owner = (jnp.arange(ATOMS, dtype=jnp.int32) // A_DEV)[:, None]
    limits = jax.random.randint(keys[0], (count,), 2, 7)
    limit_rows = jnp.repeat(limits, A_DEV)[:, None]
    chance = jax.random.randint(keys[1], (ATOMS, NB), 0, 8)
    side = jax.random.randint(keys[2], (ATOMS, NB), 0, 2) * 2 - 1
    moved = jnp.where(chance < limit_rows, side, 0)
    target = owner + moved
    moved = jnp.where((target < 0) | (target >= count), -moved, moved)
    within = jax.random.randint(keys[3], (ATOMS, NB), 0, A_DEV)
    return ((owner + moved) * A_DEV + within).astype(jnp.int32)


def draw_offsets(key, part):
    keys = jax.random.split(jax.random.fold_in(key, 23), 2)
    values = jax.random.randint(keys[0], (NQ,), 1, OMAX + 1)
    where_top = jax.random.randint(keys[1], (), 0, NQ)
    return values.at[where_top].set(OMAX).astype(jnp.int32)


def block_levels(key, extent, shards, least, top_value):
    level, own = 1.0, jax.random.fold_in(key, 6)
    for dim, shards_of in shards:
        steps = jnp.exp(jax.random.uniform(jax.random.fold_in(own, dim), (shards_of,), jnp.float32, least / len(shards), top_value / len(shards)))
        level = level * jnp.repeat(steps, extent[dim] // shards_of).reshape([-1 if axis == dim else 1 for axis in range(len(extent))])
    return level


def noise(own_key, dims, width, bound, cuts=(), kind=jnp.bfloat16):
    drawn = width * jax.random.normal(own_key, dims, jnp.float32)
    if cuts:
        drawn = drawn * block_levels(own_key, dims, cuts, -0.22, 0.18)
    return jnp.clip(drawn, -bound, bound).astype(kind)


def setup_inputs(seed: int = 0) -> dict:
    key_of = jax.random.split(jax.random.key(seed), 7)
    return {
        "green": noise(key_of[0], (ATOMS, 2, ORB, ORB, EN), 1.0, 6.0, ((0, 8), (4, 4))),
        "coupling": noise(key_of[1], (ATOMS, NB, 2, ORB, ORB), 140 ** -0.5, 0.5, ((0, 8),)),
        "neighbours": draw_neighbours(jax.random.fold_in(key_of[6], 71), 0),
        "offsets": draw_offsets(jax.random.fold_in(key_of[6], 71), 0),
        "w_emit": jnp.clip(jnp.exp(jax.random.uniform(key_of[4], (NQ,), jnp.float32, math.log(0.02), math.log(0.2))), 0.02, 0.2),
        "w_absorb": jnp.clip(jnp.exp(jax.random.uniform(key_of[5], (NQ,), jnp.float32, math.log(0.02), math.log(0.2))), 0.02, 0.2),
    }


def couple(blocks, gathered):
    hi = lax.Precision.HIGHEST
    coup = blocks.astype(jnp.float32)
    grn = gathered.astype(jnp.float32)
    x_re = jnp.einsum("kij,kjle->kile", coup[:, 0], grn[:, 0], precision=hi) - jnp.einsum("kij,kjle->kile", coup[:, 1], grn[:, 1], precision=hi)
    x_im = jnp.einsum("kij,kjle->kile", coup[:, 0], grn[:, 1], precision=hi) + jnp.einsum("kij,kjle->kile", coup[:, 1], grn[:, 0], precision=hi)
    x_re = lax.optimization_barrier(x_re.astype(jnp.bfloat16)).astype(jnp.float32)
    x_im = lax.optimization_barrier(x_im.astype(jnp.bfloat16)).astype(jnp.float32)
    p_re = jnp.einsum("kile,kml->ime", x_re, coup[:, 0], precision=hi) + jnp.einsum("kile,kml->ime", x_im, coup[:, 1], precision=hi)
    p_im = jnp.einsum("kile,kml->ime", x_im, coup[:, 0], precision=hi) - jnp.einsum("kile,kml->ime", x_re, coup[:, 1], precision=hi)
    return jnp.stack([p_re, p_im])


def reference(green, coupling, neighbours, offsets, w_emit, w_absorb):
    shifts = jnp.arange(-OMAX, OMAX + 1, dtype=jnp.int32)
    coeffs = jnp.sum(jnp.where(offsets[None, :] == shifts[:, None], w_emit[None, :], jnp.float32(0.0)), axis=1)
    coeffs = coeffs + jnp.sum(jnp.where(-offsets[None, :] == shifts[:, None], w_absorb[None, :], jnp.float32(0.0)), axis=1)

    def one_atom(packed):
        blocks, listed = packed
        gathered = jnp.take(green, listed, axis=0)
        coupled = couple(blocks, gathered).reshape(-1, EN)
        padded = jnp.pad(coupled, ((0, 0), (OMAX, OMAX)))

        def add_shift(index, total):
            return total + coeffs[index] * lax.dynamic_slice_in_dim(padded, index, EN, 1)

        total = lax.fori_loop(0, 2 * OMAX + 1, add_shift, jnp.zeros_like(coupled))
        return total.reshape(2, ORB, ORB, EN)

    return lax.map(one_atom, (coupling, neighbours))
```

```python
import jax
import jax.numpy as jnp
from jax import lax
from jax.experimental import pallas as pl
from jax.experimental.pallas import tpu as pltpu
from jax.sharding import PartitionSpec as P

F32 = jnp.float32
BF16 = jnp.bfloat16
ROWS = 16


def shifted(value, axis, step):
    count = lax.axis_size(axis)
    pairs = [(i, i + step) for i in range(count) if 0 <= i + step < count]
    return lax.ppermute(value, axis, pairs)


def expanders(orb, width):
    half = width // 2
    row = lax.broadcasted_iota(jnp.int32, (2 * ROWS, width), 0)
    col = lax.broadcasted_iota(jnp.int32, (2 * ROWS, width), 1)
    part = (row >= ROWS).astype(jnp.int32)
    entry = row - ROWS * part
    side = (col >= half).astype(jnp.int32)
    outer = (col >> 4) - orb * side
    inner = col & 15
    one, zero = jnp.float32(1), jnp.float32(0)
    at_outer, at_inner = entry == outer, entry == inner
    a1 = jnp.where(at_outer & (part == side), one, zero)
    a2 = jnp.where(at_outer & (part != side), jnp.where(side == 0, one, -one), zero)
    b1 = jnp.where(at_inner & (part == 0), one, zero)
    b2 = jnp.where(at_inner & (part == 1), one, zero)
    return [m.astype(BF16) for m in (a1, a2, b1, b2)]


def build(nb_ref, coup_ref, l_ref, a1_ref, a2_ref, b1_ref, b2_ref, acc_ref):
    atoms, listed = nb_ref.shape
    near, orb, _, width = acc_ref.shape
    first = (lax.axis_index("atom") - 1) * atoms
    mats = expanders(orb, width)
    for a in range(atoms):
        for ref, mat in zip((a1_ref, a2_ref, b1_ref, b2_ref), mats):
            ref[...] = jnp.dot(coup_ref[a], mat, preferred_element_type=F32).reshape(ref.shape)
        acc_ref[...] = jnp.zeros_like(acc_ref)

        def one(k, carry):
            b = nb_ref[a, k] - first
            b1, b2 = b1_ref[k], b2_ref[k]
            for i in range(orb):
                acc_ref[b, i] += a1_ref[k, i : i + 1, :] * b1 + a2_ref[k, i : i + 1, :] * b2
            return carry

        lax.fori_loop(0, listed, one, 0)
        for b in range(near):
            l_ref[a, :, :, b * width : (b + 1) * width] = acc_ref[b].astype(BF16)


def split(x):
    high = x.astype(BF16)
    return high, (x - high.astype(F32)).astype(BF16)


def spread_matrix(off_ref, emit_ref, absorb_ref, points):
    span = 2 * points
    lane = lax.broadcasted_iota(jnp.int32, (8, span), 1)
    line = jnp.zeros((8, span), F32)
    for q in range(off_ref.shape[0]):
        off = off_ref[q]
        line += jnp.where(lane == span - off, emit_ref[q], jnp.float32(0))
        line += jnp.where(lane == off, absorb_ref[q], jnp.float32(0))
    full = jnp.broadcast_to(line[0:1], (points, span))
    return pltpu.roll(full, 0, 1, stride=1, stride_axis=0)


def finish(off_ref, emit_ref, absorb_ref, l_ref, lower_ref, own_ref, upper_ref, out_ref, side_ref, rhs_ref):
    atoms, _, orb, _, points = own_ref.shape
    rhs_ref[...] = jnp.zeros_like(rhs_ref)
    for g, ref in enumerate((lower_ref, own_ref, upper_ref)):
        for a in range(atoms):
            b = g * atoms + a
            re, im = ref[a, 0], ref[a, 1]
            rhs_ref[b, 0, :, 0:orb, :points] = re
            rhs_ref[b, 0, :, 0:orb, points:] = im
            rhs_ref[b, 1, :, 0:orb, :points] = -im
            rhs_ref[b, 1, :, 0:orb, points:] = re
    rows = atoms * orb * ROWS
    depth = l_ref.shape[-1]
    p = jnp.dot(
        l_ref[...].reshape(rows, depth), rhs_ref[...].reshape(depth, 2 * points), preferred_element_type=F32
    )
    t_high, t_low = split(spread_matrix(off_ref, emit_ref, absorb_ref, points))
    for r in range(2):
        high, low = split(p[:, r * points : (r + 1) * points])
        s = jnp.dot(high, t_high, preferred_element_type=F32)
        s += jnp.dot(high, t_low, preferred_element_type=F32)
        s += jnp.dot(low, t_high, preferred_element_type=F32)
        s = s.reshape(atoms, orb, ROWS, 2 * points)
        for a in range(atoms):
            out_ref[a, r] = s[a, :, :orb, :points]
            side_ref[a, r] = s[a, :, :orb, points:].astype(BF16)


def shards(green, coupling, neighbours, offsets, w_emit, w_absorb):
    atoms, _, orb, _, points = green.shape
    listed = neighbours.shape[1]
    reach = points * 3 // 8
    width = 2 * orb * ROWS
    near = 3 * atoms
    vmem, smem = pl.BlockSpec(memory_space=pltpu.VMEM), pl.BlockSpec(memory_space=pltpu.SMEM)
    lower = shifted(green, "atom", 1)
    upper = shifted(green, "atom", -1)
    coup = jnp.pad(
        coupling.transpose(0, 1, 3, 2, 4), ((0, 0), (0, 0), (0, ROWS - orb), (0, 0), (0, ROWS - orb))
    ).reshape(atoms, listed * ROWS, 2 * ROWS)
    expanded = pltpu.VMEM((listed, ROWS, width), F32)
    operator = pl.pallas_call(
        build,
        out_shape=jax.ShapeDtypeStruct((atoms, orb, ROWS, near * width), BF16),
        in_specs=[smem, vmem],
        out_specs=vmem,
        scratch_shapes=[expanded] * 4 + [pltpu.VMEM((near, orb, ROWS, width), F32)],
        compiler_params=pltpu.CompilerParams(vmem_limit_bytes=32 << 20),
        cost_estimate=pl.CostEstimate(flops=30_000_000, bytes_accessed=12_000_000, transcendentals=0),
    )(neighbours, coup)
    result, side = pl.pallas_call(
        finish,
        out_shape=(
            jax.ShapeDtypeStruct(green.shape, F32),
            jax.ShapeDtypeStruct(green.shape, BF16),
        ),
        in_specs=[smem, smem, smem] + [vmem] * 4,
        out_specs=(vmem, vmem),
        scratch_shapes=[pltpu.VMEM((near, 2, orb, ROWS, 2 * points), BF16)],
        compiler_params=pltpu.CompilerParams(vmem_limit_bytes=32 << 20),
    )(offsets, w_emit, w_absorb, operator, lower, green, upper)
    from_lower = shifted(side, "energy", 1)
    from_upper = shifted(side, "energy", -1)
    lane = jnp.arange(points, dtype=jnp.int32)
    result += jnp.where(lane < reach, from_lower, 0).astype(F32)
    return result + jnp.where(lane >= points - reach, from_upper, 0).astype(F32)


def solution(mesh):
    return jax.shard_map(
        shards,
        mesh=mesh,
        in_specs=(
            P("atom", None, None, None, "energy"),
            P("atom", None, None, None, None),
            P("atom", None),
            P(),
            P(),
            P(),
        ),
        out_specs=P("atom", None, None, None, "energy"),
        check_vma=False,
    )
```

```python
import jax
import jax.numpy as jnp
from jax import lax
from jax.experimental import pallas as pl
from jax.experimental.pallas import tpu as pltpu
from jax.sharding import PartitionSpec as P

F32 = jnp.float32
BF16 = jnp.bfloat16
PAD = 16
CHUNKS = 4


def expanders(orb, width):
    row = lax.broadcasted_iota(jnp.int32, (2 * orb, width), 0)
    col = lax.broadcasted_iota(jnp.int32, (2 * orb, width), 1)
    outer = lax.div(col, 2 * orb)
    inner = lax.div(col - outer * 2 * orb, 2)
    side = col & 1
    part, entry = row & 1, row >> 1
    one, zero = jnp.float32(1), jnp.float32(0)
    at_outer, at_inner = entry == outer, entry == inner
    a1 = jnp.where(at_outer & (part == 0), one, zero)
    a2 = jnp.where(at_outer & (part == 1), one, zero)
    b1 = jnp.where(at_inner & (part == side), one, zero)
    b2 = jnp.where(at_inner & (part != side), jnp.where(side == 0, one, -one), zero)
    return [m.astype(BF16) for m in (a1, a2, b1, b2)]


def split(x):
    high = x.astype(BF16)
    return high, (x - high.astype(F32)).astype(BF16)


def spread_matrix(off_ref, emit_ref, absorb_ref, points):
    span = 2 * points
    lane = lax.broadcasted_iota(jnp.int32, (8, span), 1)

    def add(q, line):
        off = off_ref[q]
        line += jnp.where(lane == span - off, emit_ref[q], jnp.float32(0))
        return line + jnp.where(lane == off, absorb_ref[q], jnp.float32(0))

    line = lax.fori_loop(0, off_ref.shape[0], add, jnp.zeros((8, span), F32))
    full = jnp.broadcast_to(line[0:1], (points, span))
    return pltpu.roll(full, 0, 1, stride=1, stride_axis=0)


def kernel(
    count_a, count_e, orb, listed,
    nb_ref, off_ref, emit_ref, absorb_ref, green_ref, coup_ref,
    out_ref,
    recv_ref, a1_ref, a2_ref, b1_ref, b2_ref, sums_ref, op_ref, toep_ref, side_ref, got_ref,
    near_send, near_recv, far_send, far_recv, side_send, side_recv,
):
    rows, points = green_ref.shape
    width = 2 * orb * orb
    atoms = rows // width
    near = 3 * atoms
    reach = points * 3 // 8
    mine, energy = lax.axis_index("atom"), lax.axis_index("energy")
    odd = lax.rem(mine, 2)
    partner = mine + 1 - 2 * odd
    target = mine + 2 - 4 * odd
    source = mine - 2 + 4 * odd
    has_target = (target >= 0) & (target < count_a)
    has_source = (source >= 0) & (source < count_a)
    has_lower, has_upper = energy > 0, energy < count_e - 1

    barrier = pltpu.get_barrier_semaphore()

    def greet(atom, point):
        pl.semaphore_signal(barrier, inc=1, device_id=(atom, point), device_id_type=pl.DeviceIdType.MESH)

    greet(partner, energy)
    pl.when(has_target)(lambda: greet(target, energy))
    pl.when(has_source)(lambda: greet(source, energy))
    pl.when(has_lower)(lambda: greet(mine, energy - 1))
    pl.when(has_upper)(lambda: greet(mine, energy + 1))
    expected = 1
    for there in (has_target, has_source, has_lower, has_upper):
        expected += there.astype(jnp.int32)
    pl.semaphore_wait(barrier, expected)

    def remote(src, dst, send, recv, atom, point):
        return pltpu.make_async_remote_copy(
            src_ref=src, dst_ref=dst, send_sem=send, recv_sem=recv,
            device_id=(atom, point), device_id_type=pl.DeviceIdType.MESH,
        )

    size = rows // CHUNKS
    near_copies, far_copies = [], []
    for c in range(CHUNKS):
        part = pl.ds(c * size, size)
        near_copies.append(remote(
            green_ref.at[part], recv_ref.at[odd, part], near_send.at[c], near_recv.at[c], partner, energy))
        far_copies.append(remote(
            recv_ref.at[1 - odd, part], recv_ref.at[odd, part], far_send.at[c], far_recv.at[c], target, energy))
    for copy in near_copies:
        copy.start()

    @pl.when(jnp.logical_not(has_source))
    def _():
        recv_ref[odd] = jnp.zeros((rows, points), BF16)

    def forward(chunks):
        for c in chunks:
            near_copies[c].wait_recv()
        for c in chunks:
            pl.when(has_target)(far_copies[c].start)

    mats = expanders(orb, width)
    over_rows = (((0,), (0,)), ((), ()))
    b1_ref[...] = jnp.zeros_like(b1_ref)
    b2_ref[...] = jnp.zeros_like(b2_ref)
    sums_ref[0] = jnp.zeros_like(sums_ref[0])
    first = (mine - 1) * atoms
    for a in range(atoms):
        for i in range(orb):
            start = (a * orb + i) * 2 * orb
            entries = coup_ref[start : start + 2 * orb, :]
            wide = [lax.dot_general(entries, m, over_rows, preferred_element_type=F32) for m in mats]
            a1_ref[i], a2_ref[i] = wide[0], wide[1]
            b1_ref[:, i, :], b2_ref[:, i, :] = wide[2], wide[3]

        def one(k, last):
            b = nb_ref[a, k] - first
            before = jnp.int32(0)
            for x in range(near):
                before = jnp.where(b == x, last[x], before)
            b1, b2 = b1_ref[k], b2_ref[k]
            for i in range(orb):
                sums_ref[k + 1, i] = (
                    sums_ref[before, i] + a1_ref[i, pl.ds(k, 1), :] * b1 + a2_ref[i, pl.ds(k, 1), :] * b2
                )
            return tuple(jnp.where(b == x, k + 1, last[x]) for x in range(near))

        last = (jnp.int32(0),) * near
        last = lax.fori_loop(0, listed // 2, one, last)
        if a == atoms - 1:
            forward(range(CHUNKS // 2, CHUNKS))
        last = lax.fori_loop(listed // 2, listed, one, last)
        for x in range(near):
            op_ref[x, a] = sums_ref[last[x]].astype(BF16)
        if a == 0:
            forward(range(CHUNKS // 2 if atoms > 1 else CHUNKS))
    toep_ref[...] = spread_matrix(off_ref, emit_ref, absorb_ref, points)

    row = lax.broadcasted_iota(jnp.int32, (width, width), 0)
    col = lax.broadcasted_iota(jnp.int32, (width, width), 1)
    even = (row & 1) == 0
    turn = jnp.where(even, (col == row + 1).astype(F32), -(col == row - 1).astype(F32)).astype(BF16)
    height = atoms * orb * PAD

    def apply(block, group):
        total = None
        for a in range(atoms):
            g = block(a)
            turned = jnp.dot(turn, g, preferred_element_type=F32).astype(BF16)
            op = op_ref[group * atoms + a].reshape(height, width)
            term = jnp.dot(op, jnp.concatenate([g, turned], axis=1), preferred_element_type=F32)
            total = term if total is None else total + term
        return total

    p = apply(lambda a: green_ref[a * width : (a + 1) * width], 1)
    p += apply(lambda a: recv_ref[1 - odd, a * width : (a + 1) * width], 2 - 2 * odd)
    for c in range(CHUNKS):
        pl.when(has_source)(far_copies[c].wait_recv)
    p += apply(lambda a: recv_ref[odd, a * width : (a + 1) * width], 2 * odd)

    t_high, t_low = split(toep_ref[...])
    high, low = split(p)

    def spread(r, lanes):
        cut = slice(r * points, (r + 1) * points)
        s = jnp.dot(high[:, cut], t_high[:, lanes], preferred_element_type=F32)
        s += jnp.dot(high[:, cut], t_low[:, lanes], preferred_element_type=F32)
        return s + jnp.dot(low[:, cut], t_high[:, lanes], preferred_element_type=F32)

    ends = slice(points, 2 * points)
    lane = lax.broadcasted_iota(jnp.int32, (height, points), 1)
    end_re = spread(0, ends)
    end_im = pltpu.roll(spread(1, ends), points // 2, 1)
    left = lane < points // 2
    side_ref[0] = jnp.where(left, end_re, end_im).astype(BF16)
    side_ref[1] = jnp.where(left, end_im, end_re).astype(BF16)
    go_up = remote(side_ref.at[0], got_ref.at[0], side_send.at[0], side_recv.at[0], mine, energy + 1)
    go_down = remote(side_ref.at[1], got_ref.at[1], side_send.at[1], side_recv.at[1], mine, energy - 1)
    pl.when(has_upper)(go_up.start)
    pl.when(has_lower)(go_down.start)
    results = [spread(r, slice(0, points)) for r in range(2)]
    pl.when(has_lower)(go_up.wait_recv)
    pl.when(has_upper)(go_down.wait_recv)
    low_end = jnp.where(has_lower, got_ref[0].astype(F32), jnp.float32(0))
    high_end = jnp.where(has_upper, got_ref[1].astype(F32), jnp.float32(0))
    for r in range(2):
        if r:
            low_end = pltpu.roll(low_end, points // 2, 1)
            high_end = pltpu.roll(high_end, points // 2, 1)
        total = results[r] + jnp.where(lane < reach, low_end, jnp.float32(0))
        total += jnp.where(lane >= points - reach, high_end, jnp.float32(0))
        for n in range(atoms * orb):
            out_ref[pl.ds(2 * orb * n + r, orb, stride=2), :] = total[n * PAD : n * PAD + orb]
    for c in range(CHUNKS):
        near_copies[c].wait_send()
        pl.when(has_target)(far_copies[c].wait_send)
    pl.when(has_upper)(go_up.wait_send)
    pl.when(has_lower)(go_down.wait_send)


def shards(green, coupling, neighbours, offsets, w_emit, w_absorb):
    atoms, _, orb, _, points = green.shape
    listed = neighbours.shape[1]
    width = 2 * orb * orb
    rows = atoms * width
    near = 3 * atoms
    height = atoms * orb * PAD
    vmem, smem = pl.BlockSpec(memory_space=pltpu.VMEM), pl.BlockSpec(memory_space=pltpu.SMEM)
    dma = pltpu.SemaphoreType.DMA

    def body(*refs):
        kernel(lax.axis_size("atom"), lax.axis_size("energy"), orb, listed, *refs)

    out = pl.pallas_call(
        body,
        out_shape=jax.ShapeDtypeStruct((rows, points), F32),
        in_specs=[smem] * 4 + [vmem] * 2,
        out_specs=vmem,
        scratch_shapes=[
            pltpu.VMEM((2, rows, points), BF16),
            pltpu.VMEM((orb, listed, width), F32),
            pltpu.VMEM((orb, listed, width), F32),
            pltpu.VMEM((listed, PAD, width), F32),
            pltpu.VMEM((listed, PAD, width), F32),
            pltpu.VMEM((listed + 1, orb, PAD, width), F32),
            pltpu.VMEM((near, atoms, orb, PAD, width), BF16),
            pltpu.VMEM((points, 2 * points), F32),
            pltpu.VMEM((2, height, points), BF16),
            pltpu.VMEM((2, height, points), BF16),
            dma((CHUNKS,)), dma((CHUNKS,)), dma((CHUNKS,)), dma((CHUNKS,)), dma((2,)), dma((2,)),
        ],
        compiler_params=pltpu.CompilerParams(
            collective_id=0, has_side_effects=True, vmem_limit_bytes=40 << 20
        ),
    )(
        neighbours, offsets, w_emit, w_absorb,
        green.transpose(0, 2, 3, 1, 4).reshape(rows, points),
        coupling.transpose(0, 3, 4, 2, 1).reshape(rows, listed),
    )
    return out.reshape(atoms, orb, orb, 2, points).transpose(0, 3, 1, 2, 4)


def solution(mesh):
    return jax.shard_map(
        shards,
        mesh=mesh,
        in_specs=(
            P("atom", None, None, None, "energy"),
            P("atom", None, None, None, None),
            P("atom", None),
            P(),
            P(),
            P(),
        ),
        out_specs=P("atom", None, None, None, "energy"),
        check_vma=False,
    )
```

```python
import jax
import jax.numpy as jnp
from jax import lax
from jax.experimental import pallas as pl
from jax.experimental.pallas import tpu as pltpu
from jax.sharding import PartitionSpec as P

F32 = jnp.float32
BF16 = jnp.bfloat16
PAD = 16
CHUNKS = 4
GROUP = 4


def expanders(orb, width):
    row = lax.broadcasted_iota(jnp.int32, (2 * orb, width), 0)
    col = lax.broadcasted_iota(jnp.int32, (2 * orb, width), 1)
    outer = lax.div(col, 2 * orb)
    inner = lax.div(col - outer * 2 * orb, 2)
    side = col & 1
    part, entry = row & 1, row >> 1
    one, zero = jnp.float32(1), jnp.float32(0)
    at_outer, at_inner = entry == outer, entry == inner
    a1 = jnp.where(at_outer & (part == 0), one, zero)
    a2 = jnp.where(at_outer & (part == 1), one, zero)
    b1 = jnp.where(at_inner & (part == side), one, zero)
    b2 = jnp.where(at_inner & (part != side), jnp.where(side == 0, one, -one), zero)
    return [m.astype(BF16) for m in (a1, a2, b1, b2)]


def split(x):
    high = x.astype(BF16)
    return high, (x - high.astype(F32)).astype(BF16)


def spread_matrix(off_ref, emit_ref, absorb_ref, points):
    span = 2 * points
    lane = lax.broadcasted_iota(jnp.int32, (8, span), 1)

    def add(q, line):
        off = off_ref[q]
        line += jnp.where(lane == span - off, emit_ref[q], jnp.float32(0))
        return line + jnp.where(lane == off, absorb_ref[q], jnp.float32(0))

    line = lax.fori_loop(0, off_ref.shape[0], add, jnp.zeros((8, span), F32), unroll=True)
    full = jnp.broadcast_to(line[0:1], (points, span))
    return pltpu.roll(full, 0, 1, stride=1, stride_axis=0)


def kernel(
    count_a, count_e, orb, listed,
    nb_ref, off_ref, emit_ref, absorb_ref, green_ref, coup_ref,
    out_ref,
    recv_ref, a1_ref, a2_ref, b1_ref, b2_ref, flat_ref, sums_ref, op_ref, toep_ref, side_ref, got_ref,
    near_send, near_recv, far_send, far_recv, side_send, side_recv,
):
    rows, points = green_ref.shape
    width = 2 * orb * orb
    atoms = rows // width
    near = 3 * atoms
    reach = points * 3 // 8
    mine, energy = lax.axis_index("atom"), lax.axis_index("energy")
    odd = lax.rem(mine, 2)
    partner = mine + 1 - 2 * odd
    target = mine + 2 - 4 * odd
    source = mine - 2 + 4 * odd
    has_target = (target >= 0) & (target < count_a)
    has_source = (source >= 0) & (source < count_a)
    has_lower, has_upper = energy > 0, energy < count_e - 1

    barrier = pltpu.get_barrier_semaphore()

    def greet(atom, point):
        pl.semaphore_signal(barrier, inc=1, device_id=(atom, point), device_id_type=pl.DeviceIdType.MESH)

    greet(partner, energy)
    pl.when(has_target)(lambda: greet(target, energy))
    pl.when(has_source)(lambda: greet(source, energy))
    pl.when(has_lower)(lambda: greet(mine, energy - 1))
    pl.when(has_upper)(lambda: greet(mine, energy + 1))
    expected = 1
    for there in (has_target, has_source, has_lower, has_upper):
        expected += there.astype(jnp.int32)
    pl.semaphore_wait(barrier, expected)

    def remote(src, dst, send, recv, atom, point):
        return pltpu.make_async_remote_copy(
            src_ref=src, dst_ref=dst, send_sem=send, recv_sem=recv,
            device_id=(atom, point), device_id_type=pl.DeviceIdType.MESH,
        )

    size = rows // CHUNKS
    near_copies, far_copies = [], []
    for c in range(CHUNKS):
        part = pl.ds(c * size, size)
        near_copies.append(remote(
            green_ref.at[part], recv_ref.at[odd, part], near_send.at[c], near_recv.at[c], partner, energy))
        far_copies.append(remote(
            recv_ref.at[1 - odd, part], recv_ref.at[odd, part], far_send.at[c], far_recv.at[c], target, energy))
    for copy in near_copies:
        copy.start()

    @pl.when(jnp.logical_not(has_source))
    def _():
        recv_ref[odd] = jnp.zeros((rows, points), BF16)

    def forward(chunks):
        for c in chunks:
            near_copies[c].wait_recv()
        for c in chunks:
            pl.when(has_target)(far_copies[c].start)

    mats = expanders(orb, width)
    same = lax.broadcasted_iota(jnp.int32, (2 * orb, 2 * orb), 0) == lax.broadcasted_iota(
        jnp.int32, (2 * orb, 2 * orb), 1
    )
    same = same.astype(F32).astype(BF16)
    over_rows = (((0,), (0,)), ((), ()))
    flat_ref[...] = jnp.zeros_like(flat_ref)
    sums_ref[0] = jnp.zeros_like(sums_ref[0])
    first = (mine - 1) * atoms
    for a in range(atoms):
        for i in range(orb):
            start = (a * orb + i) * 2 * orb
            entries = coup_ref[start : start + 2 * orb, :]
            flat_ref[pl.ds(i, listed, stride=PAD), :] = lax.dot_general(
                entries, same, over_rows, preferred_element_type=F32
            )
        flat = flat_ref[...].astype(BF16)
        for mat, ref in zip(mats, (a1_ref, a2_ref, b1_ref, b2_ref)):
            ref[...] = jnp.dot(flat, mat, preferred_element_type=F32).reshape(ref.shape)

        def one(k, last):
            b = nb_ref[a, k] - first
            before = jnp.int32(0)
            for x in range(near):
                before = jnp.where(b == x, last[x], before)
            b1, b2 = b1_ref[k], b2_ref[k]
            for start in range(0, orb, GROUP):
                group = range(start, min(start + GROUP, orb))
                old = [sums_ref[before, i] for i in group]
                new = [
                    o + a1_ref[k, i : i + 1, :] * b1 + a2_ref[k, i : i + 1, :] * b2 for o, i in zip(old, group)
                ]
                for i, value in zip(group, new):
                    sums_ref[k + 1, i] = value
            return tuple(jnp.where(b == x, k + 1, last[x]) for x in range(near))

        last = (jnp.int32(0),) * near
        last = lax.fori_loop(0, listed // 2, one, last)
        if a == atoms - 1:
            forward(range(CHUNKS // 2, CHUNKS))
        last = lax.fori_loop(listed // 2, listed, one, last)
        for x in range(near):
            op_ref[x, a] = sums_ref[last[x]].astype(BF16)
        if a == 0:
            forward(range(CHUNKS // 2 if atoms > 1 else CHUNKS))
    toep_ref[...] = spread_matrix(off_ref, emit_ref, absorb_ref, points)

    row = lax.broadcasted_iota(jnp.int32, (width, width), 0)
    col = lax.broadcasted_iota(jnp.int32, (width, width), 1)
    even = (row & 1) == 0
    turn = jnp.where(even, (col == row + 1).astype(F32), -(col == row - 1).astype(F32)).astype(BF16)
    height = atoms * orb * PAD

    def apply(block, group):
        total = None
        for a in range(atoms):
            g = block(a)
            turned = jnp.dot(turn, g, preferred_element_type=F32).astype(BF16)
            op = op_ref[group * atoms + a].reshape(height, width)
            term = jnp.dot(op, jnp.concatenate([g, turned], axis=1), preferred_element_type=F32)
            total = term if total is None else total + term
        return total

    p = apply(lambda a: green_ref[a * width : (a + 1) * width], 1)
    p += apply(lambda a: recv_ref[1 - odd, a * width : (a + 1) * width], 2 - 2 * odd)
    for c in range(CHUNKS):
        pl.when(has_source)(far_copies[c].wait_recv)
    p += apply(lambda a: recv_ref[odd, a * width : (a + 1) * width], 2 * odd)

    t_high, t_low = split(toep_ref[...])
    high, low = split(p)

    def spread(r, lanes):
        cut = slice(r * points, (r + 1) * points)
        s = jnp.dot(high[:, cut], t_high[:, lanes], preferred_element_type=F32)
        s += jnp.dot(high[:, cut], t_low[:, lanes], preferred_element_type=F32)
        return s + jnp.dot(low[:, cut], t_high[:, lanes], preferred_element_type=F32)

    ends = slice(points, 2 * points)
    lane = lax.broadcasted_iota(jnp.int32, (height, points), 1)
    end_re = spread(0, ends)
    end_im = pltpu.roll(spread(1, ends), points // 2, 1)
    left = lane < points // 2
    side_ref[0] = jnp.where(left, end_re, end_im).astype(BF16)
    side_ref[1] = jnp.where(left, end_im, end_re).astype(BF16)
    go_up = remote(side_ref.at[0], got_ref.at[0], side_send.at[0], side_recv.at[0], mine, energy + 1)
    go_down = remote(side_ref.at[1], got_ref.at[1], side_send.at[1], side_recv.at[1], mine, energy - 1)
    pl.when(has_upper)(go_up.start)
    pl.when(has_lower)(go_down.start)
    results = [spread(r, slice(0, points)) for r in range(2)]
    pl.when(has_lower)(go_up.wait_recv)
    pl.when(has_upper)(go_down.wait_recv)
    low_end = jnp.where(has_lower, got_ref[0].astype(F32), jnp.float32(0))
    high_end = jnp.where(has_upper, got_ref[1].astype(F32), jnp.float32(0))
    for r in range(2):
        if r:
            low_end = pltpu.roll(low_end, points // 2, 1)
            high_end = pltpu.roll(high_end, points // 2, 1)
        total = results[r] + jnp.where(lane < reach, low_end, jnp.float32(0))
        total += jnp.where(lane >= points - reach, high_end, jnp.float32(0))
        for n in range(atoms * orb):
            out_ref[pl.ds(2 * orb * n + r, orb, stride=2), :] = total[n * PAD : n * PAD + orb]
    for c in range(CHUNKS):
        near_copies[c].wait_send()
        pl.when(has_target)(far_copies[c].wait_send)
    pl.when(has_upper)(go_up.wait_send)
    pl.when(has_lower)(go_down.wait_send)


def shards(green, coupling, neighbours, offsets, w_emit, w_absorb):
    atoms, _, orb, _, points = green.shape
    listed = neighbours.shape[1]
    width = 2 * orb * orb
    rows = atoms * width
    near = 3 * atoms
    height = atoms * orb * PAD
    vmem, smem = pl.BlockSpec(memory_space=pltpu.VMEM), pl.BlockSpec(memory_space=pltpu.SMEM)
    dma = pltpu.SemaphoreType.DMA

    def body(*refs):
        kernel(lax.axis_size("atom"), lax.axis_size("energy"), orb, listed, *refs)

    out = pl.pallas_call(
        body,
        out_shape=jax.ShapeDtypeStruct((rows, points), F32),
        in_specs=[smem] * 4 + [vmem] * 2,
        out_specs=vmem,
        scratch_shapes=[
            pltpu.VMEM((2, rows, points), BF16),
            pltpu.VMEM((listed, PAD, width), F32),
            pltpu.VMEM((listed, PAD, width), F32),
            pltpu.VMEM((listed, PAD, width), F32),
            pltpu.VMEM((listed, PAD, width), F32),
            pltpu.VMEM((listed * PAD, 2 * orb), F32),
            pltpu.VMEM((listed + 1, orb, PAD, width), F32),
            pltpu.VMEM((near, atoms, orb, PAD, width), BF16),
            pltpu.VMEM((points, 2 * points), F32),
            pltpu.VMEM((2, height, points), BF16),
            pltpu.VMEM((2, height, points), BF16),
            dma((CHUNKS,)), dma((CHUNKS,)), dma((CHUNKS,)), dma((CHUNKS,)), dma((2,)), dma((2,)),
        ],
        compiler_params=pltpu.CompilerParams(
            collective_id=0, has_side_effects=True, vmem_limit_bytes=40 << 20
        ),
    )(
        neighbours, offsets, w_emit, w_absorb,
        green.transpose(0, 2, 3, 1, 4).reshape(rows, points),
        coupling.transpose(0, 3, 4, 2, 1).reshape(rows, listed),
    )
    return out.reshape(atoms, orb, orb, 2, points).transpose(0, 3, 1, 2, 4)


def solution(mesh):
    return jax.shard_map(
        shards,
        mesh=mesh,
        in_specs=(
            P("atom", None, None, None, "energy"),
            P("atom", None, None, None, None),
            P("atom", None),
            P(),
            P(),
            P(),
        ),
        out_specs=P("atom", None, None, None, "energy"),
        check_vma=False,
    )
```
